32 devices in a mesh: row: 8 (over y, x, core), col: 4 (over z).
Axes of the slice: x: 2, y: 2, z: 4, core: 2. Of those that a mesh axis runs over, the one named last changes fastest.
Arguments:
- perturbation: bfloat16 [16384, 16384], P('row', 'col'), may hold values from -0.046875 to 0.046875
- basis: bfloat16 [16384, 16384], P('row', 'col'), may hold values from -0.125 to 0.125
- orbitals: bfloat16 [16384, 512], P('col', 'row'), may hold values from -6 to 6
- pair_mask: int32 [16384, 512], P('col'), may hold values 0 or 1
- energies: float32 [16384], P('col'), may hold values from 1 to 4
- occ_energies: float32 [512], replicated, may hold values from -3 to -1
Outputs:
- response: float32 [16384, 512], P('row', 'col')
The draws below stay inside these ranges and needn't reach their ends.
All inputs are finite; a program needn't handle non-finite values. No bound on the sum of `pair_mask` on one device may be relied on, other than what follows from the above.
Results may differ from the reference program's by a relative error of at most 0.0037.
Values may be sent and summed in bfloat16 or wider, within the bound.
A program may use at most 128 MiB of HBM per device.

```python
import jax
import jax.numpy as jnp

M = 16384
NOCC = 512


def touch_ends(array, rng, least, top_value):
    place = [jax.random.randint(jax.random.fold_in(rng, axis), (), 0, length) for axis, length in enumerate(array.shape)]
    main_axis = array.shape.index(max(array.shape))
    next_to = place[:main_axis] + [(place[main_axis] + 1) % array.shape[main_axis]] + place[main_axis + 1:]
    return array.at[tuple(place)].set(least).at[tuple(next_to)].set(top_value)


def steps_of(rng, dims, cuts, low, high):
    factor_of, own = 1.0, jax.random.fold_in(rng, 6)
    for axis_at, blocks in cuts:
        heights = jnp.exp(jax.random.uniform(jax.random.fold_in(own, axis_at), (blocks,), jnp.float32, low / len(cuts), high / len(cuts)))
        factor_of = factor_of * jnp.repeat(heights, dims[axis_at] // blocks).reshape([-1 if axis == axis_at else 1 for axis in range(len(dims))])
    return factor_of


def noise(rng, shape, spread, bound, pieces=(), dtype=jnp.bfloat16):
    gain = steps_of(rng, shape, pieces, -0.22, 0.18) if pieces else 1.0
    result = jax.random.normal(rng, shape, jnp.float32) * spread * gain
    return jnp.minimum(jnp.maximum(result, -bound), bound).astype(dtype)


def setup_inputs(seed: int = 0) -> dict:
    arg_keys = jax.random.split(jax.random.key(seed), 7)
    perturbation = noise(arg_keys[0], (M, M), M ** -0.5, 0.046875, ((0, 8), (1, 4)))
    basis = noise(arg_keys[1], (M, M), (M // 8) ** -0.5, 0.125, ((0, 8), (1, 4)))
    orbitals = noise(arg_keys[2], (M, NOCC), 1.0, 6.0, ((0, 4), (1, 8)))
    pair_mask = touch_ends((jax.random.randint(arg_keys[3], (M, NOCC), 0, 4) < 3).astype(jnp.int32), jax.random.fold_in(arg_keys[3], 1), 0, 1)
    energies = jnp.clip(1.0 + 3.0 * jax.random.uniform(arg_keys[4], (M,), jnp.float32) ** steps_of(arg_keys[4], (M,), ((0, 4),), -0.2, 0.2), 1.0, 4.0)
    occ_energies = jnp.clip(jax.random.uniform(arg_keys[5], (NOCC,), jnp.float32, -3.0, -1.0), -3.0, -1.0)
    return dict(perturbation=perturbation, basis=basis, orbitals=orbitals, pair_mask=pair_mask, energies=energies, occ_energies=occ_energies)


def reference(perturbation, basis, orbitals, pair_mask, energies, occ_energies):
    image = jnp.dot(perturbation, orbitals, preferred_element_type=jnp.float32).astype(jnp.bfloat16)
    projection = jnp.dot(basis.T, image, preferred_element_type=jnp.float32)
    spacing = energies[:, None] - occ_energies[None, :]
    coefficients = jnp.where(pair_mask == 1, projection / spacing, jnp.zeros_like(projection)).astype(jnp.bfloat16)
    return jnp.dot(basis, coefficients, preferred_element_type=jnp.float32)
```

```python
import functools

import jax
import jax.numpy as jnp
from jax import lax
from jax.experimental import pallas as pl
from jax.experimental.pallas import tpu as pltpu
from jax.sharding import PartitionSpec as P

MESH = pl.DeviceIdType.MESH
F32, BF16 = jnp.float32, jnp.bfloat16
NT = (((1,), (1,)), ((), ()))


def plan(nr, nc, rows, cols, width):
    chunks = max(1, min(4, width // 16))
    unit = width // chunks
    tile = min(512, rows)
    bits = nr.bit_length() - 1
    assert 1 << bits == nr and nr % nc == 0
    return chunks, unit, tile, rows // tile, bits


def kernel(nr, nc, sizes, hop, fhop, gaps, x_hbm, p_hbm, b_hbm, w_ref, out_ref,
           xg, pt, bv, yown, lr, rr, ls, rs, img, proj, drecv, fp, fl, fr, fs,
           x_sem, p_sem, b_sem, ag_s, ag_r, d_s, d_r, l_s, l_r, r_s, r_r, f_s, fl_r, fr_r):
    chunks, unit, tile, tiles, bits = sizes
    rows, cols = bv.shape
    steps_b = chunks * tiles
    q = nr // nc
    me, z = lax.axis_index("row"), lax.axis_index("col")
    ring = yown.shape[0]

    def bit_values(odd):
        order = list(range(bits - 1, 0, -1)) if odd else list(range(1, bits))
        return [1 << b for b in order + [0]]

    even_bits, odd_bits = bit_values(False), bit_values(True)

    def place(d, odd):
        even_at = sum(((d // v) % 2) * (1 << t) for t, v in enumerate(even_bits))
        odd_at = sum(((d // v) % 2) * (1 << t) for t, v in enumerate(odd_bits))
        return jnp.where(odd == 1, odd_at, even_at)

    def peer(t, odd):
        ve, vo = even_bits[t], odd_bits[t]
        pe = me + (1 - 2 * ((me // ve) % 2)) * ve
        po = me + (1 - 2 * ((me // vo) % 2)) * vo
        return jnp.where(odd == 1, po, pe)

    def at_unit(u, n=1):
        return pl.ds(pl.multiple_of(u * unit, unit), n * unit)

    def gather_copy(which, k, t):
        odd = k % 2
        base = (place(me, odd) // (1 << t)) * (1 << t)
        block = xg.at[k, at_unit(base, 1 << t)]
        return pltpu.make_async_remote_copy(
            block, block, ag_s.at[which, k, t], ag_r.at[which, k, t],
            device_id=(peer(t, odd), z), device_id_type=MESH)

    def halves(k, t):
        at = place(me, k % 2)
        base = (at // (2 << t)) * (2 << t)
        bit = (at // (1 << t)) % 2
        return base + bit * (1 << t), base + (1 - bit) * (1 << t)

    def reduce_copy(k, t):
        _, away = halves(k, t)
        return pltpu.make_async_remote_copy(
            proj.at[k % 2, at_unit(away, 1 << t)],
            drecv.at[k, pl.ds(((1 << t) - 1) * unit, (1 << t) * unit)],
            d_s.at[k, t], d_r.at[k, t], device_id=(peer(t, k % 2), z), device_id_type=MESH)

    def right_copy(j):
        return pltpu.make_async_remote_copy(
            rs.at[j], lr.at[j], r_s.at[j], l_r.at[j], device_id=(me, jnp.minimum(z + 1, nc - 1)), device_id_type=MESH)

    def left_copy(j):
        return pltpu.make_async_remote_copy(
            ls.at[j], rr.at[j], l_s.at[j], r_r.at[j], device_id=(me, jnp.maximum(z - 1, 0)), device_id_type=MESH)

    def f_right(k, c):
        return pltpu.make_async_remote_copy(
            fs.at[k, c], fl.at[k, c], f_s.at[k, c], fl_r.at[k, c],
            device_id=(me, jnp.minimum(z + 1, nc - 1)), device_id_type=MESH)

    def f_left(k, c):
        return pltpu.make_async_remote_copy(
            fs.at[k, c], fr.at[k, c], f_s.at[k, c], fr_r.at[k, c],
            device_id=(me, jnp.maximum(z - 1, 0)), device_id_type=MESH)

    def p_copy(s):
        return pltpu.make_async_copy(
            p_hbm.at[pl.ds(pl.multiple_of((s % tiles) * tile, tile), tile)], pt.at[s % 2], p_sem.at[s % 2])

    def x_copy(k):
        return pltpu.make_async_copy(
            x_hbm.at[pl.ds(k * unit, unit)], xg.at[k, at_unit(place(me, k % 2))], x_sem.at[k])

    b_copy = pltpu.make_async_copy(b_hbm, bv, b_sem)

    for k in range(chunks):
        x_copy(k).start()
    p_copy(0).start()

    barrier = pltpu.get_barrier_semaphore()
    for b in range(bits):
        other = me + (1 - 2 * ((me // (1 << b)) % 2)) * (1 << b)
        pl.semaphore_signal(barrier, inc=1, device_id=(other, z), device_id_type=MESH)

    @pl.when(z > 0)
    def _():
        pl.semaphore_signal(barrier, inc=1, device_id=(me, jnp.maximum(z - 1, 0)), device_id_type=MESH)

    @pl.when(z < nc - 1)
    def _():
        pl.semaphore_signal(barrier, inc=1, device_id=(me, jnp.minimum(z + 1, nc - 1)), device_id_type=MESH)

    pl.semaphore_wait(barrier, bits + jnp.minimum(z, 1) + jnp.minimum(nc - 1 - z, 1))

    for k in range(chunks):
        x_copy(k).wait()
        gather_copy(0, k, 0).start()
    b_copy.start()

    def gather_step(which, k, t):
        gather_copy(which, k, t).wait()
        if t + 1 < bits:
            gather_copy(which, k, t + 1).start()

    for t in range(bits):
        gather_step(0, 0, t)

    def image_tile(s):
        p_copy(s).wait()

        @pl.when(s + 1 < steps_b)
        def _():
            p_copy(s + 1).start()

        yown[s % ring] = lax.dot_general(xg[s // tiles], pt[s % 2], NT, preferred_element_type=F32)

    def pass_right(j):
        @pl.when(z == 0)
        def _():
            rs[j] = yown[j % ring].astype(BF16)

        @pl.when(z > 0)
        def _():
            right_copy(j).wait_recv()

        @pl.when(jnp.logical_and(z > 0, z < nc - 1))
        def _():
            rs[j] = (yown[j % ring] + lr[j].astype(F32)).astype(BF16)

        @pl.when(z < nc - 1)
        def _():
            right_copy(j).start()

    def pass_left(j):
        @pl.when(z == nc - 1)
        def _():
            ls[j] = yown[j % ring].astype(BF16)

        @pl.when(z < nc - 1)
        def _():
            left_copy(j).wait_recv()

        @pl.when(jnp.logical_and(z > 0, z < nc - 1))
        def _():
            ls[j] = (yown[j % ring] + rr[j].astype(F32)).astype(BF16)

        @pl.when(z > 0)
        def _():
            left_copy(j).start()

    def image_done(j):
        @pl.when(z > 0)
        def _():
            yown[j % ring] += lr[j].astype(F32)

        @pl.when(z < nc - 1)
        def _():
            yown[j % ring] += rr[j].astype(F32)

        k, t = j // tiles, j % tiles
        img[k % 2, :, pl.ds(pl.multiple_of(t * tile, tile), tile)] = yown[j % ring].astype(BF16)

    ctile = min(512, cols)

    def project(k):
        @pl.when(k == 0)
        def _():
            b_copy.wait()

        def body(i, carry):
            at = pl.ds(pl.multiple_of(i * ctile, ctile), ctile)
            proj[k % 2, :, at] = jnp.dot(img[k % 2], bv[:, at], preferred_element_type=F32)
            return carry

        lax.fori_loop(0, cols // ctile, body, 0)
        reduce_copy(k, bits - 1).start()

    def reduce_step(k, t):
        reduce_copy(k, t).wait()
        keep, _ = halves(k, t)
        at = at_unit(keep, 1 << t)
        got = drecv[k, pl.ds(((1 << t) - 1) * unit, (1 << t) * unit)]
        if t > 0:
            proj[k % 2, at] += got
            reduce_copy(k, t - 1).start()
        else:
            coef = (proj[k % 2, at] + got) * w_ref[pl.ds(pl.multiple_of(k * unit, unit), unit)]
            xg[k, at] = coef.astype(BF16)
            gather_copy(1, k, 0).start()

    def respond(k):
        def body(i, carry):
            at = pl.ds(pl.multiple_of(i * tile, tile), tile)
            fp[k % 2, :, at] = lax.dot_general(xg[k], bv[at], NT, preferred_element_type=F32)
            return carry

        lax.fori_loop(0, rows // tile, body, 0)

    def share(k, c, i):
        return fp[k % 2, at_unit(place(c * q + i, k % 2))]

    def out_right(k):
        for c in range(nc - 1, 0, -1):
            @pl.when(jnp.logical_and(z == 0, c > z))
            def _():
                for i in range(q):
                    fs[k, c, i * unit:(i + 1) * unit] = share(k, c, i).astype(BF16)

            @pl.when(jnp.logical_and(z > 0, c > z))
            def _():
                f_right(k, c).wait_recv()
                for i in range(q):
                    at = slice(i * unit, (i + 1) * unit)
                    fs[k, c, at] = (share(k, c, i) + fl[k, c, at].astype(F32)).astype(BF16)

            @pl.when(c > z)
            def _():
                f_right(k, c).start()

    def out_left(k):
        for c in range(nc - 1):
            @pl.when(jnp.logical_and(z == nc - 1, c < z))
            def _():
                for i in range(q):
                    fs[k, c, i * unit:(i + 1) * unit] = share(k, c, i).astype(BF16)

            @pl.when(jnp.logical_and(z < nc - 1, c < z))
            def _():
                f_left(k, c).wait_recv()
                for i in range(q):
                    at = slice(i * unit, (i + 1) * unit)
                    fs[k, c, at] = (share(k, c, i) + fr[k, c, at].astype(F32)).astype(BF16)

            @pl.when(c < z)
            def _():
                f_left(k, c).start()

    def out_done(k):
        for i in range(q):
            out_ref[k, i] = share(k, z, i)

        @pl.when(z > 0)
        def _():
            f_right(k, z).wait_recv()
            for i in range(q):
                out_ref[k, i] += fl[k, z, i * unit:(i + 1) * unit].astype(F32)

        @pl.when(z < nc - 1)
        def _():
            f_left(k, z).wait_recv()
            for i in range(q):
                out_ref[k, i] += fr[k, z, i * unit:(i + 1) * unit].astype(F32)

    def each(s, offset, task):
        d = s - offset
        k = d // tiles

        @pl.when(jnp.logical_and(d >= 0, jnp.logical_and(d % tiles == 0, k < chunks)))
        def _():
            task(k)

    def tile_task(s, lag, task):
        j = s - lag

        @pl.when(jnp.logical_and(j >= 0, j < steps_b))
        def _():
            task(j)

    reduce_gaps, gather_gaps = gaps
    at_project = tiles - 1 + hop * (nc - 1)
    timeline, now = [], at_project
    for n, t in enumerate(range(bits - 1, -1, -1)):
        now += reduce_gaps[min(n, len(reduce_gaps) - 1)]
        timeline.append((now, functools.partial(lambda t, k: reduce_step(k, t), t)))
    for t in range(bits):
        now += gather_gaps[min(t, len(gather_gaps) - 1)]
        timeline.append((now, functools.partial(lambda t, k: gather_step(1, k, t), t)))
    at_respond = now
    last = (chunks - 1) * tiles + at_respond + fhop * (nc - 1) + 1

    def step(s, carry):
        tile_task(s, 0, image_tile)
        tile_task(s, hop * z, pass_right)
        tile_task(s, hop * (nc - 1 - z), pass_left)
        tile_task(s, hop * (nc - 1), image_done)
        if chunks > 1:
            for t in range(bits):
                ahead = min(1 + t, tiles - 1)
                d = s - ahead
                k = d // tiles + 1

                @pl.when(jnp.logical_and(d >= 0, jnp.logical_and(d % tiles == 0, k < chunks)))
                def _():
                    gather_step(0, k, t)
        for offset, task in timeline:
            each(s, offset, task)
        each(s, at_project, project)
        each(s, at_respond, respond)
        each(s, at_respond + fhop * z, out_right)
        each(s, at_respond + fhop * (nc - 1 - z), out_left)
        each(s, at_respond + fhop * (nc - 1), out_done)
        return carry

    lax.fori_loop(0, last, step, 0)

    def drain(j, carry):
        @pl.when(z < nc - 1)
        def _():
            right_copy(j).wait_send()

        @pl.when(z > 0)
        def _():
            left_copy(j).wait_send()

        return carry

    lax.fori_loop(0, steps_b, drain, 0)

    def drain_out(k, carry):
        for c in range(nc):
            @pl.when(c > z)
            def _():
                f_right(k, c).wait_send()

            @pl.when(c < z)
            def _():
                f_left(k, c).wait_send()

        return carry

    lax.fori_loop(0, chunks, drain_out, 0)


def shards(perturbation, basis, orbitals, pair_mask, energies, occ_energies):
    nr, nc = lax.axis_size("row"), lax.axis_size("col")
    rows, cols = perturbation.shape
    width = orbitals.shape[1]
    sizes = plan(nr, nc, rows, cols, width)
    chunks, unit, tile, tiles, bits = sizes
    q = nr // nc
    count = nr * unit
    hop, fhop, gaps = 2, 2, ((1, 4, 2), (1, 2, 1))
    ring = hop * (nc - 1) + 1
    n = chunks * tiles

    first = lax.axis_index("row") * width
    mask_block = lax.dynamic_slice_in_dim(pair_mask, first, width, 1).T
    occ_block = lax.dynamic_slice_in_dim(occ_energies, first, width, 0)
    inverse = jnp.where(mask_block == 1, 1.0 / (energies[None, :] - occ_block[:, None]), 0.0)

    dma = pltpu.SemaphoreType.DMA
    result = pl.pallas_call(
        functools.partial(kernel, nr, nc, sizes, hop, fhop, gaps),
        out_shape=jax.ShapeDtypeStruct((chunks, q, unit, rows), F32),
        in_specs=[pl.BlockSpec(memory_space=pl.ANY)] * 3 + [pl.BlockSpec(memory_space=pltpu.VMEM)],
        out_specs=pl.BlockSpec(memory_space=pltpu.VMEM),
        scratch_shapes=[
            pltpu.VMEM((chunks, count, cols), BF16),
            pltpu.VMEM((2, tile, cols), BF16),
            pltpu.VMEM((rows, cols), BF16),
            pltpu.VMEM((ring, count, tile), F32),
            pltpu.VMEM((n, count, tile), BF16),
            pltpu.VMEM((n, count, tile), BF16),
            pltpu.VMEM((n, count, tile), BF16),
            pltpu.VMEM((n, count, tile), BF16),
            pltpu.VMEM((2, count, rows), BF16),
            pltpu.VMEM((2, count, cols), F32),
            pltpu.VMEM((chunks, (nr - 1) * unit, cols), F32),
            pltpu.VMEM((2, count, rows), F32),
            pltpu.VMEM((chunks, nc, q * unit, rows), BF16),
            pltpu.VMEM((chunks, nc, q * unit, rows), BF16),
            pltpu.VMEM((chunks, nc, q * unit, rows), BF16),
            dma((chunks,)), dma((2,)), dma,
            dma((2, chunks, bits)), dma((2, chunks, bits)),
            dma((chunks, bits)), dma((chunks, bits)),
            dma((n,)), dma((n,)), dma((n,)), dma((n,)),
            dma((chunks, nc)), dma((chunks, nc)), dma((chunks, nc)),
        ],
        compiler_params=pltpu.CompilerParams(
            collective_id=0, has_side_effects=True, vmem_limit_bytes=63 * 1024 * 1024),
    )(orbitals.T, perturbation, basis, inverse)
    return result.transpose(3, 1, 0, 2).reshape(rows, q * width)


def solution(mesh):
    return jax.shard_map(
        shards,
        mesh=mesh,
        in_specs=(P("row", "col"), P("row", "col"), P("col", "row"), P("col", None), P("col"), P()),
        out_specs=P("row", "col"),
        check_vma=False,
    )
```

```python
import functools

import jax
import jax.numpy as jnp
from jax import lax
from jax.experimental import pallas as pl
from jax.experimental.pallas import tpu as pltpu
from jax.sharding import PartitionSpec as P

MESH = pl.DeviceIdType.MESH
F32, BF16 = jnp.float32, jnp.bfloat16
NT = (((1,), (1,)), ((), ()))


def plan(nr, nc, rows, cols, width):
    chunks = max(1, min(4, width // 16))
    unit = width // chunks
    tile = min(512, rows)
    bits = nr.bit_length() - 1
    assert 1 << bits == nr and nr % nc == 0
    return chunks, unit, tile, rows // tile, bits


def kernel(nr, nc, sizes, hop, fhop, gaps, x_hbm, p_hbm, b_hbm, w_ref, out_ref,
           xg, pt, bv, yown, lr, rr, ls, rs, img, proj, drecv, fp, fl, fr, fs,
           x_sem, p_sem, b_sem, ag_s, ag_r, d_s, d_r, l_s, l_r, r_s, r_r, f_s, fl_r, fr_r):
    chunks, unit, tile, tiles, bits = sizes
    rows, cols = bv.shape
    steps_b = chunks * tiles
    q = nr // nc
    me, z = lax.axis_index("row"), lax.axis_index("col")
    ring = yown.shape[0]

    def bit_values(odd):
        order = list(range(bits - 1, 0, -1)) if odd else list(range(1, bits))
        return [1 << b for b in order + [0]]

    even_bits, odd_bits = bit_values(False), bit_values(True)

    def place(d, odd):
        even_at = sum(((d // v) % 2) * (1 << t) for t, v in enumerate(even_bits))
        odd_at = sum(((d // v) % 2) * (1 << t) for t, v in enumerate(odd_bits))
        return jnp.where(odd == 1, odd_at, even_at)

    def peer(t, odd):
        ve, vo = even_bits[t], odd_bits[t]
        pe = me + (1 - 2 * ((me // ve) % 2)) * ve
        po = me + (1 - 2 * ((me // vo) % 2)) * vo
        return jnp.where(odd == 1, po, pe)

    def at_unit(u, n=1):
        return pl.ds(pl.multiple_of(u * unit, unit), n * unit)

    def gather_copy(which, k, t):
        odd = k % 2
        base = (place(me, odd) // (1 << t)) * (1 << t)
        block = xg.at[k, at_unit(base, 1 << t)]
        return pltpu.make_async_remote_copy(
            block, block, ag_s.at[which, k, t], ag_r.at[which, k, t],
            device_id=(peer(t, odd), z), device_id_type=MESH)

    def halves(k, t):
        at = place(me, k % 2)
        base = (at // (2 << t)) * (2 << t)
        bit = (at // (1 << t)) % 2
        return base + bit * (1 << t), base + (1 - bit) * (1 << t)

    def reduce_copy(k, t):
        _, away = halves(k, t)
        return pltpu.make_async_remote_copy(
            proj.at[k % 2, at_unit(away, 1 << t)],
            drecv.at[k, pl.ds(((1 << t) - 1) * unit, (1 << t) * unit)],
            d_s.at[k, t], d_r.at[k, t], device_id=(peer(t, k % 2), z), device_id_type=MESH)

    def right_copy(j):
        return pltpu.make_async_remote_copy(
            rs.at[j], lr.at[j], r_s.at[j], l_r.at[j], device_id=(me, jnp.minimum(z + 1, nc - 1)), device_id_type=MESH)

    def left_copy(j):
        return pltpu.make_async_remote_copy(
            ls.at[j], rr.at[j], l_s.at[j], r_r.at[j], device_id=(me, jnp.maximum(z - 1, 0)), device_id_type=MESH)

    def f_right(k, c):
        return pltpu.make_async_remote_copy(
            fs.at[k, c], fl.at[k, c], f_s.at[k, c], fl_r.at[k, c],
            device_id=(me, jnp.minimum(z + 1, nc - 1)), device_id_type=MESH)

    def f_left(k, c):
        return pltpu.make_async_remote_copy(
            fs.at[k, c], fr.at[k, c], f_s.at[k, c], fr_r.at[k, c],
            device_id=(me, jnp.maximum(z - 1, 0)), device_id_type=MESH)

    def p_copy(s):
        return pltpu.make_async_copy(
            p_hbm.at[pl.ds(pl.multiple_of((s % tiles) * tile, tile), tile)], pt.at[s % 2], p_sem.at[s % 2])

    def x_copy(k):
        return pltpu.make_async_copy(
            x_hbm.at[pl.ds(k * unit, unit)], xg.at[k, at_unit(place(me, k % 2))], x_sem.at[k])

    b_copy = pltpu.make_async_copy(b_hbm, bv, b_sem)

    for k in range(chunks):
        x_copy(k).start()
    p_copy(0).start()

    barrier = pltpu.get_barrier_semaphore()
    for b in range(bits):
        other = me + (1 - 2 * ((me // (1 << b)) % 2)) * (1 << b)
        pl.semaphore_signal(barrier, inc=1, device_id=(other, z), device_id_type=MESH)

    @pl.when(z > 0)
    def _():
        pl.semaphore_signal(barrier, inc=1, device_id=(me, jnp.maximum(z - 1, 0)), device_id_type=MESH)

    @pl.when(z < nc - 1)
    def _():
        pl.semaphore_signal(barrier, inc=1, device_id=(me, jnp.minimum(z + 1, nc - 1)), device_id_type=MESH)

    pl.semaphore_wait(barrier, bits + jnp.minimum(z, 1) + jnp.minimum(nc - 1 - z, 1))

    for k in range(chunks):
        x_copy(k).wait()
        gather_copy(0, k, 0).start()
    b_copy.start()

    def gather_step(which, k, t):
        gather_copy(which, k, t).wait()
        if t + 1 < bits:
            gather_copy(which, k, t + 1).start()

    for t in range(bits):
        gather_step(0, 0, t)

    def image_tile(s):
        p_copy(s).wait()

        @pl.when(s + 1 < steps_b)
        def _():
            p_copy(s + 1).start()

        yown[s % ring] = lax.dot_general(xg[s // tiles], pt[s % 2], NT, preferred_element_type=F32)

    def pass_right(j):
        @pl.when(z == 0)
        def _():
            rs[j] = yown[j % ring].astype(BF16)

        @pl.when(z > 0)
        def _():
            right_copy(j).wait_recv()

        @pl.when(jnp.logical_and(z > 0, z < nc - 1))
        def _():
            rs[j] = (yown[j % ring] + lr[j].astype(F32)).astype(BF16)

        @pl.when(z < nc - 1)
        def _():
            right_copy(j).start()

    def pass_left(j):
        @pl.when(z == nc - 1)
        def _():
            ls[j] = yown[j % ring].astype(BF16)

        @pl.when(z < nc - 1)
        def _():
            left_copy(j).wait_recv()

        @pl.when(jnp.logical_and(z > 0, z < nc - 1))
        def _():
            ls[j] = (yown[j % ring] + rr[j].astype(F32)).astype(BF16)

        @pl.when(z > 0)
        def _():
            left_copy(j).start()

    def image_done(j):
        @pl.when(z > 0)
        def _():
            yown[j % ring] += lr[j].astype(F32)

        @pl.when(z < nc - 1)
        def _():
            yown[j % ring] += rr[j].astype(F32)

        k, t = j // tiles, j % tiles
        img[k % 2, :, pl.ds(pl.multiple_of(t * tile, tile), tile)] = yown[j % ring].astype(BF16)

    ctile = min(512, cols)

    def project(k):
        @pl.when(k == 0)
        def _():
            b_copy.wait()

        def body(i, carry):
            at = pl.ds(pl.multiple_of(i * ctile, ctile), ctile)
            proj[k % 2, :, at] = jnp.dot(img[k % 2], bv[:, at], preferred_element_type=F32)
            return carry

        lax.fori_loop(0, cols // ctile, body, 0)
        reduce_copy(k, bits - 1).start()

    def reduce_step(k, t):
        reduce_copy(k, t).wait()
        keep, _ = halves(k, t)
        at = at_unit(keep, 1 << t)
        got = drecv[k, pl.ds(((1 << t) - 1) * unit, (1 << t) * unit)]
        if t > 0:
            proj[k % 2, at] += got
            reduce_copy(k, t - 1).start()
        else:
            coef = (proj[k % 2, at] + got) * w_ref[pl.ds(pl.multiple_of(k * unit, unit), unit)]
            xg[k, at] = coef.astype(BF16)
            gather_copy(1, k, 0).start()

    def respond(k):
        def body(i, carry):
            at = pl.ds(pl.multiple_of(i * tile, tile), tile)
            fp[k % 2, :, at] = lax.dot_general(xg[k], bv[at], NT, preferred_element_type=F32)
            return carry

        lax.fori_loop(0, rows // tile, body, 0)

    def share(k, c, i):
        return fp[k % 2, at_unit(place(c * q + i, k % 2))]

    def out_right(k):
        for c in range(nc - 1, 0, -1):
            @pl.when(jnp.logical_and(z == 0, c > z))
            def _():
                for i in range(q):
                    fs[k, c, i * unit:(i + 1) * unit] = share(k, c, i).astype(BF16)

            @pl.when(jnp.logical_and(z > 0, c > z))
            def _():
                f_right(k, c).wait_recv()
                for i in range(q):
                    at = slice(i * unit, (i + 1) * unit)
                    fs[k, c, at] = (share(k, c, i) + fl[k, c, at].astype(F32)).astype(BF16)

            @pl.when(c > z)
            def _():
                f_right(k, c).start()

    def out_left(k):
        for c in range(nc - 1):
            @pl.when(jnp.logical_and(z == nc - 1, c < z))
            def _():
                for i in range(q):
                    fs[k, c, i * unit:(i + 1) * unit] = share(k, c, i).astype(BF16)

            @pl.when(jnp.logical_and(z < nc - 1, c < z))
            def _():
                f_left(k, c).wait_recv()
                for i in range(q):
                    at = slice(i * unit, (i + 1) * unit)
                    fs[k, c, at] = (share(k, c, i) + fr[k, c, at].astype(F32)).astype(BF16)

            @pl.when(c < z)
            def _():
                f_left(k, c).start()

    def out_done(k):
        for i in range(q):
            out_ref[k, i] = share(k, z, i)

        @pl.when(z > 0)
        def _():
            f_right(k, z).wait_recv()
            for i in range(q):
                out_ref[k, i] += fl[k, z, i * unit:(i + 1) * unit].astype(F32)

        @pl.when(z < nc - 1)
        def _():
            f_left(k, z).wait_recv()
            for i in range(q):
                out_ref[k, i] += fr[k, z, i * unit:(i + 1) * unit].astype(F32)

    def each(s, offset, task):
        d = s - offset
        k = d // tiles

        @pl.when(jnp.logical_and(d >= 0, jnp.logical_and(d % tiles == 0, k < chunks)))
        def _():
            task(k)

    def tile_task(s, lag, task):
        j = s - lag

        @pl.when(jnp.logical_and(j >= 0, j < steps_b))
        def _():
            task(j)

    reduce_gaps, gather_gaps = gaps
    at_project = tiles - 1 + hop * (nc - 1)
    timeline, now = [], at_project
    for n, t in enumerate(range(bits - 1, -1, -1)):
        now += reduce_gaps[min(n, len(reduce_gaps) - 1)]
        timeline.append((now, functools.partial(lambda t, k: reduce_step(k, t), t)))
    for t in range(bits):
        now += gather_gaps[min(t, len(gather_gaps) - 1)]
        timeline.append((now, functools.partial(lambda t, k: gather_step(1, k, t), t)))
    at_respond = now
    last = (chunks - 1) * tiles + at_respond + fhop * (nc - 1) + 1

    def step(s, carry):
        tile_task(s, 0, image_tile)
        tile_task(s, hop * z, pass_right)
        tile_task(s, hop * (nc - 1 - z), pass_left)
        tile_task(s, hop * (nc - 1), image_done)
        if chunks > 1:
            for t in range(bits):
                ahead = min(1 + t, tiles - 1)
                d = s - ahead
                k = d // tiles + 1

                @pl.when(jnp.logical_and(d >= 0, jnp.logical_and(d % tiles == 0, k < chunks)))
                def _():
                    gather_step(0, k, t)
        for offset, task in timeline:
            each(s, offset, task)
        each(s, at_project, project)
        each(s, at_respond, respond)
        each(s, at_respond + fhop * z, out_right)
        each(s, at_respond + fhop * (nc - 1 - z), out_left)
        each(s, at_respond + fhop * (nc - 1), out_done)
        return carry

    lax.fori_loop(0, last, step, 0)

    def drain(j, carry):
        @pl.when(z < nc - 1)
        def _():
            right_copy(j).wait_send()

        @pl.when(z > 0)
        def _():
            left_copy(j).wait_send()

        return carry

    lax.fori_loop(0, steps_b, drain, 0)

    def drain_out(k, carry):
        for c in range(nc):
            @pl.when(c > z)
            def _():
                f_right(k, c).wait_send()

            @pl.when(c < z)
            def _():
                f_left(k, c).wait_send()

        return carry

    lax.fori_loop(0, chunks, drain_out, 0)


def shards(perturbation, basis, orbitals, pair_mask, energies, occ_energies):
    nr, nc = lax.axis_size("row"), lax.axis_size("col")
    rows, cols = perturbation.shape
    width = orbitals.shape[1]
    sizes = plan(nr, nc, rows, cols, width)
    chunks, unit, tile, tiles, bits = sizes
    q = nr // nc
    count = nr * unit
    hop, fhop, gaps = 1, 1, ((1, 2, 1), (1, 1, 1))
    ring = hop * (nc - 1) + 1
    n = chunks * tiles

    first = lax.axis_index("row") * width
    mask_block = lax.dynamic_slice_in_dim(pair_mask, first, width, 1).T
    occ_block = lax.dynamic_slice_in_dim(occ_energies, first, width, 0)
    inverse = jnp.where(mask_block == 1, 1.0 / (energies[None, :] - occ_block[:, None]), 0.0)

    dma = pltpu.SemaphoreType.DMA
    result = pl.pallas_call(
        functools.partial(kernel, nr, nc, sizes, hop, fhop, gaps),
        out_shape=jax.ShapeDtypeStruct((chunks, q, unit, rows), F32),
        in_specs=[pl.BlockSpec(memory_space=pl.ANY)] * 3 + [pl.BlockSpec(memory_space=pltpu.VMEM)],
        out_specs=pl.BlockSpec(memory_space=pltpu.VMEM),
        scratch_shapes=[
            pltpu.VMEM((chunks, count, cols), BF16),
            pltpu.VMEM((2, tile, cols), BF16),
            pltpu.VMEM((rows, cols), BF16),
            pltpu.VMEM((ring, count, tile), F32),
            pltpu.VMEM((n, count, tile), BF16),
            pltpu.VMEM((n, count, tile), BF16),
            pltpu.VMEM((n, count, tile), BF16),
            pltpu.VMEM((n, count, tile), BF16),
            pltpu.VMEM((2, count, rows), BF16),
            pltpu.VMEM((2, count, cols), F32),
            pltpu.VMEM((chunks, (nr - 1) * unit, cols), F32),
            pltpu.VMEM((2, count, rows), F32),
            pltpu.VMEM((chunks, nc, q * unit, rows), BF16),
            pltpu.VMEM((chunks, nc, q * unit, rows), BF16),
            pltpu.VMEM((chunks, nc, q * unit, rows), BF16),
            dma((chunks,)), dma((2,)), dma,
            dma((2, chunks, bits)), dma((2, chunks, bits)),
            dma((chunks, bits)), dma((chunks, bits)),
            dma((n,)), dma((n,)), dma((n,)), dma((n,)),
            dma((chunks, nc)), dma((chunks, nc)), dma((chunks, nc)),
        ],
        compiler_params=pltpu.CompilerParams(
            collective_id=0, has_side_effects=True, vmem_limit_bytes=63 * 1024 * 1024),
    )(orbitals.T, perturbation, basis, inverse)
    return result.transpose(3, 1, 0, 2).reshape(rows, q * width)


def solution(mesh):
    return jax.shard_map(
        shards,
        mesh=mesh,
        in_specs=(P("row", "col"), P("row", "col"), P("col", "row"), P("col", None), P("col"), P()),
        out_specs=P("row", "col"),
        check_vma=False,
    )
```
